512 devices in a mesh: dp: 32 (over y, x), feat: 16 (over z, core).
Axes of the slice: x: 4, y: 8, z: 8, core: 2. Of those that a mesh axis runs over, the one named last changes fastest.
Arguments:
- data: bfloat16 [98304, 4096], P('dp', 'feat'), may hold values from -6 to 6
- block_counts: int32 [32], replicated, may hold values from 1 to 6, 64 in all
- basis: bfloat16 [4096, 256], P('feat'), may hold values from -0.09375 to 0.09375
Outputs:
- basis_scaled: float32 [4096, 256], P('feat')
- upper: float32 [256, 256], replicated
The draws below stay inside these ranges and needn't reach their ends.
Inputs may be any that keep to these rules, and one draw needn't show every extreme that they name: `block_counts`: every index of dp has one or more valid blocks, the counts sum to 2 * 32, and the largest is exactly 6.
All inputs are finite; a program needn't handle non-finite values.
Results may differ from the reference program's by a relative error of at most 0.00065.
Values may be sent and summed in bfloat16 or wider, within the bound.
No kernel may reach another device: no remote copies, remote signals or barrier semaphores. Data moves between devices by JAX's collectives and lax.ppermute only.
A program may use at most 64 MiB of HBM per device.

```python
import math
import jax
import jax.numpy as jnp
import numpy as np
from jax import lax

D = 4096
K = 256
BLOCK = 512
MEAN_BLK = 2
CAP_BLK = 6
ROWS_CAP = 3072
ROWS_ALL = 98304
N_DP = 32


def block_scale(key, extent, cuts, low, largest):
    def one(position, shards_of):
        steps = jax.random.uniform(jax.random.fold_in(jax.random.fold_in(key, 6), position), (shards_of,), jnp.float32, low / len(cuts), largest / len(cuts))
        return jnp.repeat(jnp.exp(steps), extent[position] // shards_of).reshape((-1,) + (1,) * (len(extent) - position - 1))

    level = one(*cuts[0])
    for cut in cuts[1:]:
        level = level * one(*cut)
    return level


def split_up(number_of, total, most, slope):
    loads = [(1 << 20) // math.isqrt(standing ** slope) + 1 for standing in range(2, number_of + 1)]
    surplus, holding = total - most - (number_of - 1), [1] * (number_of - 1)
    while surplus > 0:
        candidates = [i for i in range(number_of - 1) if holding[i] < most]
        mass, budget = sum([loads[i] for i in candidates]), surplus
        for i in candidates:
            addition = min(most - holding[i], max(1, budget * loads[i] // mass), surplus)
            holding[i] = holding[i] + addition
            surplus = surplus - addition
    return np.array([most] + holding)


def uneven_parts(own_key, count, total, bound, lean):
    if count == 2:
        one = jax.random.randint(own_key, (), max(1, total - bound), min(bound, total - 1) + 1)
        return jnp.stack([one, total - one])
    lengths = jnp.asarray(split_up(count, total, bound, lean), jnp.int32)
    couples = (count - 1) // 2
    giver, sink = lengths[1:1 + 2 * couples:2], lengths[2:2 + 2 * couples:2]
    room = jnp.minimum(giver - 1, bound - sink)
    passed = jax.random.randint(jax.random.fold_in(own_key, 1), (couples,), 0, 1 << 20) % (room + 1)
    lengths = lengths.at[1:1 + 2 * couples:2].set(giver - passed).at[2:2 + 2 * couples:2].set(sink + passed)
    return lengths[jax.random.permutation(jax.random.fold_in(own_key, 2), count)]


def scatter_about(own_key, dims, scale, most, split=(), held_as=jnp.bfloat16):
    drawn = scale * jax.random.normal(own_key, dims, jnp.float32)
    if split:
        drawn = drawn * block_scale(own_key, dims, split, -0.22, 0.18)
    return jnp.clip(drawn, -most, most).astype(held_as)


def setup_inputs(seed: int = 0) -> dict:
    key_of = jax.random.split(jax.random.key(seed), 4)
    return {
        "data": scatter_about(key_of[0], (ROWS_ALL, D), 1.0, 6.0, ((0, 32), (1, 16))),
        "block_counts": uneven_parts(key_of[1], N_DP, MEAN_BLK * N_DP, CAP_BLK, 2).astype(jnp.int32),
        "basis": scatter_about(key_of[2], (D, K), D ** -0.5, 0.09375, ((0, 16),)),
    }


def reference(data, block_counts, basis):
    shards = data.reshape(N_DP, ROWS_CAP, D)
    limits = (block_counts * BLOCK).astype(jnp.int32)
    row_ids = jnp.arange(ROWS_CAP, dtype=jnp.int32)

    def one_shard(total, inputs):
        shard, limit = inputs
        images = jnp.dot(shard.astype(jnp.float32), basis.astype(jnp.float32), preferred_element_type=jnp.float32).astype(jnp.bfloat16)
        images = jnp.where((row_ids < limit)[:, None], images, jnp.zeros_like(images))
        return (total + jnp.dot(shard.T.astype(jnp.float32), images.astype(jnp.float32), preferred_element_type=jnp.float32), None)
    terms, unused = lax.scan(one_shard, jnp.zeros((D, K), jnp.float32), (shards, limits))
    row_total = (jnp.sum(block_counts) * BLOCK).astype(jnp.float32)
    updated = basis.astype(jnp.float32) + terms / row_total
    factor_q, factor_r = jnp.linalg.qr(updated)
    signs = jnp.where(jnp.diagonal(factor_r) < 0, -1.0, 1.0).astype(jnp.float32)
    scaled = factor_q * signs[None, :] * math.sqrt(D)
    return (scaled.astype(jnp.float32), (factor_r * signs[:, None]).astype(jnp.float32))
```

```python
import math

import jax
import jax.numpy as jnp
from jax import lax
from jax.sharding import PartitionSpec as P

D = 4096
BLOCK = 512
CORES = 2
X = 4
F32 = jnp.float32
BF16 = jnp.bfloat16


def core_swap(value):
    count = lax.axis_size("feat")
    return lax.ppermute(value, "feat", [(i, i ^ 1) for i in range(count)])


def groups_z():
    count = lax.axis_size("feat")
    return [list(range(c, count, CORES)) for c in range(CORES)]


def groups_x():
    count = lax.axis_size("dp")
    return [list(range(y, y + X, 1)) for y in range(0, count, X)]


def spread(value, axis, groups, size):
    copies = jnp.broadcast_to(value[None], (size,) + value.shape)
    return lax.all_to_all(copies, axis, 0, 0, axis_index_groups=groups)


def sum_images(partial, feat):
    core = feat % CORES
    chips = lax.axis_size("feat") // CORES
    rows, rank = partial.shape
    split = partial.reshape(chips, CORES, rows // (chips * CORES), rank)
    mine = lax.dynamic_index_in_dim(split, core, 1, False)
    other = lax.dynamic_index_in_dim(split, 1 - core, 1, False)
    pair = mine + core_swap(other)
    pieces = lax.all_to_all(
        pair.astype(jnp.float16), "feat", 0, 0, axis_index_groups=groups_z()
    )
    return jnp.sum(pieces.astype(F32), axis=0)


def sum_gram(gram, dp, feat):
    core = feat % CORES
    chips = lax.axis_size("feat") // CORES
    rank = gram.shape[0]
    split = gram.reshape(X, CORES, rank // (X * CORES), rank)
    split = lax.dynamic_index_in_dim(split, dp % X, 0, False)
    mine = lax.dynamic_index_in_dim(split, core, 0, False)
    other = lax.dynamic_index_in_dim(split, 1 - core, 0, False)
    pair = mine + core_swap(other)
    total = jnp.sum(spread(pair, "feat", groups_z(), chips), axis=0)
    quarter = spread(total, "dp", groups_x(), X)
    theirs = core_swap(quarter)
    first = jnp.where(core == 0, quarter, theirs)
    second = jnp.where(core == 0, theirs, quarter)
    return jnp.stack([first, second], axis=1).reshape(rank, rank)


def orthonormal(matrix, dp, feat):
    local_gram = jnp.dot(matrix.T, matrix, precision=lax.Precision.HIGHEST)
    gram_total = sum_gram(local_gram, dp, feat)
    lower = jnp.linalg.cholesky(gram_total)
    solved = jax.scipy.linalg.solve_triangular(lower, matrix.T, lower=True)
    return (solved.T, lower.T)


def on_device(data, block_counts, basis):
    rows, columns = data.shape
    rank = basis.shape[1]
    dp = lax.axis_index("dp")
    feat = lax.axis_index("feat")
    dp_size = lax.axis_size("dp")
    active = lax.dynamic_index_in_dim(block_counts, dp, 0, False)

    partial = jnp.dot(data, basis, preferred_element_type=F32)
    images = sum_images(partial, feat)
    here = images.shape[0]
    row_ids = feat * here + lax.broadcasted_iota(jnp.int32, (here, 1), 0)
    images = jnp.where(row_ids < active * BLOCK, images, 0.0).astype(BF16)
    images = lax.all_gather(images, "feat", tiled=True)

    terms = lax.dot_general(
        data, images, (((0,), (0,)), ((), ())), preferred_element_type=F32
    )
    pieces = lax.all_to_all(terms.reshape(dp_size, columns // dp_size, rank), "dp", 0, 0)
    piece = jnp.sum(pieces, axis=0)
    summed_terms = spread(piece, "dp", None, dp_size).reshape(columns, rank)

    row_total = (jnp.sum(block_counts) * BLOCK).astype(F32)
    updated = basis.astype(F32) + summed_terms / row_total
    first_basis, upper_one = orthonormal(updated, dp, feat)
    second_basis, upper_two = orthonormal(first_basis, dp, feat)
    upper = jnp.dot(upper_two, upper_one, precision=lax.Precision.HIGHEST)
    return (second_basis * math.sqrt(D), upper)


def solution(mesh):
    in_specs = (P("dp", "feat"), P(), P("feat", None))
    out_specs = (P("feat", None), P())
    return jax.shard_map(
        on_device, mesh=mesh, in_specs=in_specs, out_specs=out_specs, check_vma=False
    )
```

```python
import functools
import math

import jax
import jax.numpy as jnp
from jax import lax
from jax.experimental import pallas as pl
from jax.experimental.pallas import tpu as pltpu
from jax.sharding import PartitionSpec as P

D = 4096
BLOCK = 512
CORES = 2
X = 4
F32 = jnp.float32
BF16 = jnp.bfloat16
F16 = jnp.float16

LIFT = 16.0
FLOOR = 1e-4
CLOSE = 4e-6
STEPS = 14

PLAIN = (((1,), (0,)), ((), ()))
OUTER = (((1,), (1,)), ((), ()))


def core_swap(value):
    count = lax.axis_size("feat")
    return lax.ppermute(value, "feat", [(i, i ^ 1) for i in range(count)])


def groups_z():
    count = lax.axis_size("feat")
    return [list(range(c, count, CORES)) for c in range(CORES)]


def groups_x():
    count = lax.axis_size("dp")
    return [list(range(y, y + X)) for y in range(0, count, X)]


def spread(value, axis, groups, size):
    copies = jnp.broadcast_to(value[None], (size,) + value.shape)
    return lax.all_to_all(copies, axis, 0, 0, axis_index_groups=groups)


def sum_images(partial, feat):
    core = feat % CORES
    chips = lax.axis_size("feat") // CORES
    rows, rank = partial.shape
    split = partial.reshape(chips, CORES, rows // (chips * CORES), rank)
    mine = lax.dynamic_index_in_dim(split, core, 1, False)
    other = lax.dynamic_index_in_dim(split, 1 - core, 1, False)
    pair = mine + core_swap(other)
    pieces = lax.all_to_all(
        (pair * LIFT).astype(F16), "feat", 0, 0, axis_index_groups=groups_z()
    )
    return jnp.sum(pieces.astype(F32), axis=0)


def sum_gram(gram, dp, feat):
    core = feat % CORES
    chips = lax.axis_size("feat") // CORES
    rank = gram.shape[0]
    split = gram.reshape(X, CORES, rank // (X * CORES), rank)
    split = lax.dynamic_index_in_dim(split, dp % X, 0, False)
    mine = lax.dynamic_index_in_dim(split, core, 0, False)
    other = lax.dynamic_index_in_dim(split, 1 - core, 0, False)
    pair = mine + core_swap(other)
    total = jnp.sum(spread(pair, "feat", groups_z(), chips), axis=0)
    quarter = spread(total, "dp", groups_x(), X)
    theirs = core_swap(quarter)
    first = jnp.where(core == 0, quarter, theirs)
    second = jnp.where(core == 0, theirs, quarter)
    return jnp.stack([first, second], axis=1).reshape(rank, rank)


def halves(value):
    high = value.astype(BF16)
    return high, (value - high.astype(F32)).astype(BF16)


def product(left, right, dims):
    dot = functools.partial(
        lax.dot_general, dimension_numbers=dims, preferred_element_type=F32
    )
    return dot(left[0], right[0]) + (dot(left[0], right[1]) + dot(left[1], right[0]))


def factor_kernel(gram_ref, matrix_ref, basis_ref, upper_ref, done_ref, inverse):
    gram = gram_ref[...]
    row = lax.broadcasted_iota(jnp.int32, gram.shape, 0)
    col = lax.broadcasted_iota(jnp.int32, gram.shape, 1)
    diagonal = jnp.where(row == col, gram, 0.0)
    norms = jnp.sum(diagonal, axis=0, keepdims=True)
    scale_down = lax.rsqrt(jnp.sum(diagonal, axis=1, keepdims=True))
    scale_across = lax.rsqrt(norms)
    unit = gram * scale_down * scale_across
    eye = jnp.where(row == col, 1.0, 0.0)
    keep = jnp.where(row > col, 1.0, jnp.where(row == col, 0.5, 0.0))
    unit_parts = halves(unit)
    inverse[...] = eye - (unit - eye) * keep

    def improve():
        now = inverse[...]
        parts = halves(now)
        moved = product(parts, unit_parts, PLAIN)
        excess = product(halves(moved), parts, OUTER) - eye
        inverse[...] = now - product(halves(excess * keep), parts, PLAIN)
        return jnp.sum(excess * excess)

    improve()
    _, error = lax.while_loop(
        lambda state: jnp.logical_and(state[0] < STEPS, jnp.logical_not(state[1] < CLOSE)),
        lambda state: (state[0] + 1, improve()),
        (2, improve()),
    )
    parts = halves(inverse[...])
    upper = product(parts, unit_parts, PLAIN) / scale_across
    upper_ref[...] = jnp.where(row <= col, upper, 0.0)
    matrix = matrix_ref[...] * scale_across
    basis_ref[...] = product(halves(matrix), parts, OUTER) * math.sqrt(D)
    done = jnp.logical_and(error < CLOSE, jnp.min(norms) > FLOOR)
    done_ref[0] = jnp.where(done, 1, 0)


def factor(gram, matrix):
    whole = jax.ShapeDtypeStruct(gram.shape, F32)
    vmem = pl.BlockSpec(memory_space=pltpu.VMEM)
    return pl.pallas_call(
        factor_kernel,
        out_shape=(whole, whole, jax.ShapeDtypeStruct((1,), jnp.int32)),
        in_specs=[vmem, vmem],
        out_specs=(vmem, vmem, pl.BlockSpec(memory_space=pltpu.SMEM)),
        scratch_shapes=[pltpu.VMEM(gram.shape, F32)],
        compiler_params=pltpu.CompilerParams(vmem_limit_bytes=32 * 1024 * 1024),
        name="factor",
    )(gram, matrix)


def orthonormal(matrix):
    local_gram = jnp.dot(matrix.T, matrix, precision=lax.Precision.HIGHEST)
    gram_total = lax.psum(local_gram, "feat")
    lower = jnp.linalg.cholesky(gram_total)
    solved = jax.scipy.linalg.solve_triangular(lower, matrix.T, lower=True)
    return (solved.T, lower.T)


def general(data, block_counts, basis):
    rows, rank = data.shape[0], basis.shape[1]
    active = lax.dynamic_index_in_dim(block_counts, lax.axis_index("dp"), 0, False)
    valid = lax.broadcasted_iota(jnp.int32, (rows, 1), 0) < active * BLOCK
    partial = jnp.dot(data, basis, preferred_element_type=F32)
    images = lax.psum(jnp.where(valid, partial, 0.0), "feat").astype(BF16)
    terms = lax.dot_general(
        data, images, (((0,), (0,)), ((), ())), preferred_element_type=F32
    )
    row_total = (jnp.sum(block_counts) * BLOCK).astype(F32)
    updated = basis.astype(F32) + lax.psum(terms, "dp") / row_total
    first_basis, upper_one = orthonormal(updated)
    second_basis, upper_two = orthonormal(first_basis)
    upper = jnp.dot(upper_two, upper_one, precision=lax.Precision.HIGHEST)
    return (second_basis * math.sqrt(D), upper)


def on_device(data, block_counts, basis):
    rows, columns = data.shape
    rank = basis.shape[1]
    dp = lax.axis_index("dp")
    feat = lax.axis_index("feat")
    dp_size = lax.axis_size("dp")
    active = lax.dynamic_index_in_dim(block_counts, dp, 0, False)

    partial = jnp.dot(data, basis, preferred_element_type=F32)
    images = sum_images(partial, feat)
    here = images.shape[0]
    row_ids = feat * here + lax.broadcasted_iota(jnp.int32, (here, 1), 0)
    images = jnp.where(row_ids < active * BLOCK, images, 0.0).astype(F16)
    images = lax.all_gather(images, "feat", tiled=True).astype(BF16)

    terms = lax.dot_general(
        data, images, (((0,), (0,)), ((), ())), preferred_element_type=F32
    )
    pieces = lax.all_to_all(terms.reshape(dp_size, columns // dp_size, rank), "dp", 0, 0)
    piece = jnp.sum(pieces, axis=0)
    summed_terms = spread(piece, "dp", None, dp_size).reshape(columns, rank)

    row_total = (jnp.sum(block_counts) * BLOCK).astype(F32) * LIFT
    updated = basis.astype(F32) + summed_terms / row_total
    local_gram = jnp.dot(updated.T, updated, precision=lax.Precision.HIGHEST)
    basis_scaled, upper, done = factor(sum_gram(local_gram, dp, feat), updated)
    return lax.cond(
        done[0] == 1,
        lambda: (basis_scaled, upper),
        lambda: general(data, block_counts, basis),
    )


def solution(mesh):
    in_specs = (P("dp", "feat"), P(), P("feat", None))
    out_specs = (P("feat", None), P())
    return jax.shard_map(
        on_device, mesh=mesh, in_specs=in_specs, out_specs=out_specs, check_vma=False
    )
```

```python
import functools
import math

import jax
import jax.numpy as jnp
from jax import lax
from jax.experimental import pallas as pl
from jax.experimental.pallas import tpu as pltpu
from jax.sharding import PartitionSpec as P

D = 4096
BLOCK = 512
CORES = 2
X = 4
F32 = jnp.float32
BF16 = jnp.bfloat16
F16 = jnp.float16

LIFT = 16.0
FLOOR = 1e-4
CLOSE = 4e-6
STEPS = 14

PLAIN = (((1,), (0,)), ((), ()))
OUTER = (((1,), (1,)), ((), ()))


def core_swap(value):
    count = lax.axis_size("feat")
    return lax.ppermute(value, "feat", [(i, i ^ 1) for i in range(count)])


def groups_z():
    count = lax.axis_size("feat")
    return [list(range(c, count, CORES)) for c in range(CORES)]


def groups_x():
    count = lax.axis_size("dp")
    return [list(range(y, y + X)) for y in range(0, count, X)]


def spread(value, axis, groups, size):
    copies = jnp.broadcast_to(value[None], (size,) + value.shape)
    return lax.all_to_all(copies, axis, 0, 0, axis_index_groups=groups)


def sum_images(data, basis, core, other):
    chips = lax.axis_size("feat") // CORES
    rows, columns = data.shape
    split = data.reshape(chips, CORES, rows // (chips * CORES), columns)

    def part(which):
        picked = lax.dynamic_index_in_dim(split, which, 1, False)
        return lax.dot_general(
            picked, basis, (((2,), (0,)), ((), ())), preferred_element_type=F32
        )

    pair = part(core) + core_swap(part(other))
    pieces = lax.all_to_all(
        (pair * LIFT).astype(F16), "feat", 0, 0, axis_index_groups=groups_z()
    )
    return jnp.sum(pieces.astype(F32), axis=0)


def sum_gram(gram, first_core, low_pair, even):
    chips = lax.axis_size("feat") // CORES
    rank = gram.shape[0]
    split = gram.reshape(X, CORES, rank // (X * CORES), rank)
    low = jnp.where(even, split[0], split[1])
    high = jnp.where(even, split[2], split[3])
    split = jnp.where(low_pair, low, high)
    mine = jnp.where(first_core, split[0], split[1])
    theirs = jnp.where(first_core, split[1], split[0])
    pair = mine + core_swap(theirs)
    total = jnp.sum(spread(pair, "feat", groups_z(), chips), axis=0)
    half = spread(total, "dp", groups_x(), X)
    theirs = core_swap(half)
    first = jnp.where(first_core, half, theirs)
    second = jnp.where(first_core, theirs, half)
    return jnp.stack([first, second], axis=1).reshape(rank, rank)


def halves(value):
    high = value.astype(BF16)
    return high, (value - high.astype(F32)).astype(BF16)


def product(left, right, dims):
    dot = functools.partial(
        lax.dot_general, dimension_numbers=dims, preferred_element_type=F32
    )
    return dot(left[0], right[0]) + (dot(left[0], right[1]) + dot(left[1], right[0]))


def factor_kernel(gram_ref, matrix_ref, basis_ref, upper_ref, done_ref, inverse):
    gram = gram_ref[...]
    row = lax.broadcasted_iota(jnp.int32, gram.shape, 0)
    col = lax.broadcasted_iota(jnp.int32, gram.shape, 1)
    diagonal = jnp.where(row == col, gram, 0.0)
    norms = jnp.sum(diagonal, axis=0, keepdims=True)
    scale_down = lax.rsqrt(jnp.sum(diagonal, axis=1, keepdims=True))
    scale_across = lax.rsqrt(norms)
    unit = gram * scale_down * scale_across
    eye = jnp.where(row == col, 1.0, 0.0)
    keep = jnp.where(row > col, 1.0, jnp.where(row == col, 0.5, 0.0))
    unit_parts = halves(unit)
    inverse[...] = eye - (unit - eye) * keep

    def improve():
        now = inverse[...]
        parts = halves(now)
        moved = product(parts, unit_parts, PLAIN)
        excess = product(halves(moved), parts, OUTER) - eye
        inverse[...] = now - product(halves(excess * keep), parts, PLAIN)
        return jnp.sum(excess * excess)

    improve()
    _, error = lax.while_loop(
        lambda state: jnp.logical_and(state[0] < STEPS, jnp.logical_not(state[1] < CLOSE)),
        lambda state: (state[0] + 1, improve()),
        (2, improve()),
    )
    parts = halves(inverse[...])
    upper = product(parts, unit_parts, PLAIN) / scale_across
    upper_ref[...] = jnp.where(row <= col, upper, 0.0)
    matrix = matrix_ref[...] * scale_across
    basis_ref[...] = product(halves(matrix), parts, OUTER) * math.sqrt(D)
    done = jnp.logical_and(error < CLOSE, jnp.min(norms) > FLOOR)
    done_ref[0] = jnp.where(done, 1, 0)


def factor(gram, matrix):
    whole = jax.ShapeDtypeStruct(gram.shape, F32)
    vmem = pl.BlockSpec(memory_space=pltpu.VMEM)
    return pl.pallas_call(
        factor_kernel,
        out_shape=(whole, whole, jax.ShapeDtypeStruct((1,), jnp.int32)),
        in_specs=[vmem, vmem],
        out_specs=(vmem, vmem, pl.BlockSpec(memory_space=pltpu.SMEM)),
        scratch_shapes=[pltpu.VMEM(gram.shape, F32)],
        compiler_params=pltpu.CompilerParams(vmem_limit_bytes=32 * 1024 * 1024),
        name="factor",
    )(gram, matrix)


def orthonormal(matrix):
    local_gram = jnp.dot(matrix.T, matrix, precision=lax.Precision.HIGHEST)
    gram_total = lax.psum(local_gram, "feat")
    lower = jnp.linalg.cholesky(gram_total)
    solved = jax.scipy.linalg.solve_triangular(lower, matrix.T, lower=True)
    return (solved.T, lower.T)


def general(data, block_counts, basis):
    rows, rank = data.shape[0], basis.shape[1]
    active = lax.dynamic_index_in_dim(block_counts, lax.axis_index("dp"), 0, False)
    valid = lax.broadcasted_iota(jnp.int32, (rows, 1), 0) < active * BLOCK
    partial = jnp.dot(data, basis, preferred_element_type=F32)
    images = lax.psum(jnp.where(valid, partial, 0.0), "feat").astype(BF16)
    terms = lax.dot_general(
        data, images, (((0,), (0,)), ((), ())), preferred_element_type=F32
    )
    row_total = (jnp.sum(block_counts) * BLOCK).astype(F32)
    updated = basis.astype(F32) + lax.psum(terms, "dp") / row_total
    first_basis, upper_one = orthonormal(updated)
    second_basis, upper_two = orthonormal(first_basis)
    upper = jnp.dot(upper_two, upper_one, precision=lax.Precision.HIGHEST)
    return (second_basis * math.sqrt(D), upper)


def on_device(data, block_counts, basis):
    rows, columns = data.shape
    rank = basis.shape[1]
    dp = lax.axis_index("dp")
    feat = lax.axis_index("feat")
    dp_size = lax.axis_size("dp")
    core = feat % CORES
    here = rows // lax.axis_size("feat")
    active = lax.dynamic_index_in_dim(block_counts, dp, 0, False)
    row_ids = feat * here + lax.broadcasted_iota(jnp.int32, (here, 1), 0)
    valid = jnp.where(row_ids < active * BLOCK, 1.0, 0.0)
    row_total = (jnp.sum(block_counts) * BLOCK).astype(F32)
    places = (core, 1 - core, core == 0, dp % X < 2, dp % 2 == 0)
    data, basis, valid, row_total, places = lax.optimization_barrier(
        (data, basis, valid, row_total, places)
    )
    core, other, first_core, low_pair, even = places

    images = sum_images(data, basis, core, other)
    images = (images * valid).astype(F16)
    images = lax.all_gather(images, "feat", tiled=True).astype(BF16)

    terms = lax.dot_general(
        data, images, (((0,), (0,)), ((), ())), preferred_element_type=F32
    )
    terms = (terms / row_total).astype(F16)
    pieces = lax.all_to_all(terms.reshape(dp_size, columns // dp_size, rank), "dp", 0, 0)
    piece = jnp.sum(pieces.astype(F32), axis=0) / LIFT
    step = spread(piece, "dp", None, dp_size).reshape(columns, rank)
    updated = basis.astype(F32) + step
    local_gram = jnp.dot(updated.T, updated, precision=lax.Precision.HIGHEST)
    basis_scaled, upper, done = factor(sum_gram(local_gram, first_core, low_pair, even), updated)
    return lax.cond(
        done[0] == 1,
        lambda: (basis_scaled, upper),
        lambda: general(data, block_counts, basis),
    )


def solution(mesh):
    in_specs = (P("dp", "feat"), P(), P("feat", None))
    out_specs = (P("feat", None), P())
    return jax.shard_map(
        on_device, mesh=mesh, in_specs=in_specs, out_specs=out_specs, check_vma=False
    )
```

```python
import functools
import math

import jax
import jax.numpy as jnp
from jax import lax
from jax.experimental import pallas as pl
from jax.experimental.pallas import tpu as pltpu
from jax.sharding import PartitionSpec as P

D = 4096
BLOCK = 512
CORES = 2
X = 4
F32 = jnp.float32
BF16 = jnp.bfloat16
F16 = jnp.float16

LIFT = 16.0
FLOOR = 1e-4
CLOSE = 4e-6
STEPS = 14

PLAIN = (((1,), (0,)), ((), ()))
ROWS = (((0,), (0,)), ((), ()))
OUTER = (((1,), (1,)), ((), ()))


def core_swap(value):
    count = lax.axis_size("feat")
    return lax.ppermute(value, "feat", [(i, i ^ 1) for i in range(count)])


def groups_z():
    count = lax.axis_size("feat")
    return [list(range(c, count, CORES)) for c in range(CORES)]


def groups_xc():
    count, width = lax.axis_size("dp"), lax.axis_size("feat")
    return [
        [(y + x) * width + z + c for x in range(X) for c in range(CORES)]
        for y in range(0, count, X)
        for z in range(0, width, CORES)
    ]


def spread(value, axis, groups, size):
    copies = jnp.broadcast_to(value[None], (size,) + value.shape)
    return lax.all_to_all(copies, axis, 0, 0, axis_index_groups=groups)


def total(value, axis):
    size = lax.axis_size(axis)
    pieces = lax.all_to_all(
        value.reshape((size, value.shape[0] // size) + value.shape[1:]), axis, 0, 0
    )
    return spread(jnp.sum(pieces, axis=0), axis, None, size).reshape(value.shape)


def sum_images(data, basis, core, beside):
    chips = lax.axis_size("feat") // CORES
    rows, columns = data.shape
    split = data.reshape(chips, CORES, rows // (chips * CORES), columns)

    def part(which):
        picked = lax.dynamic_index_in_dim(split, which, 1, False)
        return lax.dot_general(
            picked, basis, (((2,), (0,)), ((), ())), preferred_element_type=F32
        )

    theirs = core_swap((part(1 - core) * LIFT).astype(F16))
    mine, theirs, beside = lax.optimization_barrier((part(core), theirs, beside))
    pieces = lax.all_to_all(
        (mine * LIFT + theirs.astype(F32)).astype(F16),
        "feat",
        0,
        0,
        axis_index_groups=groups_z(),
    )
    return jnp.sum(pieces.astype(F32), axis=0), beside


def gram_kernel(place_ref, step_ref, basis_ref, updated_ref, mine_ref, theirs_ref, packed):
    updated = basis_ref[...].astype(F32) + step_ref[...]
    updated_ref[...] = updated
    half = packed.shape[0]
    share = mine_ref.shape[0]
    dot = functools.partial(
        lax.dot_general,
        dimension_numbers=ROWS,
        precision=lax.Precision.HIGHEST,
        preferred_element_type=F32,
    )
    packed[:, : 2 * half] = dot(updated[:, :half], updated)
    packed[:, 2 * half :] = dot(updated[:, half:], updated[:, half:])
    first = place_ref[0] * CORES
    mine = pl.multiple_of((first + place_ref[1]) * share, share)
    theirs = pl.multiple_of((first + 1 - place_ref[1]) * share, share)
    mine_ref[...] = packed[pl.ds(mine, share), :]
    theirs_ref[...] = packed[pl.ds(theirs, share), :]


def gram_share(place, step, basis):
    rank = basis.shape[1]
    half = rank // 2
    share = jax.ShapeDtypeStruct((half // (X * CORES), rank + half), F32)
    vmem = pl.BlockSpec(memory_space=pltpu.VMEM)
    return pl.pallas_call(
        gram_kernel,
        out_shape=(jax.ShapeDtypeStruct(basis.shape, F32), share, share),
        in_specs=[pl.BlockSpec(memory_space=pltpu.SMEM), vmem, vmem],
        out_specs=(vmem, vmem, vmem),
        scratch_shapes=[pltpu.VMEM((half, rank + half), F32)],
        compiler_params=pltpu.CompilerParams(vmem_limit_bytes=32 * 1024 * 1024),
        name="gram_share",
    )(place, step, basis)


def sum_gram(mine, theirs):
    chips = lax.axis_size("feat") // CORES
    pair = mine + core_swap(theirs)
    summed = jnp.sum(spread(pair, "feat", groups_z(), chips), axis=0)
    shares = spread(summed, ("dp", "feat"), groups_xc(), X * CORES)
    return shares.reshape(-1, shares.shape[-1])


def halves(value):
    high = value.astype(BF16)
    return high, (value - high.astype(F32)).astype(BF16)


def product(left, right, dims):
    dot = functools.partial(
        lax.dot_general, dimension_numbers=dims, preferred_element_type=F32
    )
    return dot(left[0], right[0]) + (dot(left[0], right[1]) + dot(left[1], right[0]))


def factor_kernel(packed_ref, matrix_ref, basis_ref, upper_ref, done_ref, inverse):
    half = packed_ref.shape[0]
    inverse[:half, :] = packed_ref[:, : 2 * half]
    inverse[half:, :half] = packed_ref[:, half : 2 * half].T
    inverse[half:, half:] = packed_ref[:, 2 * half :]
    gram = inverse[...]
    row = lax.broadcasted_iota(jnp.int32, gram.shape, 0)
    col = lax.broadcasted_iota(jnp.int32, gram.shape, 1)
    diagonal = jnp.where(row == col, gram, 0.0)
    norms = jnp.sum(diagonal, axis=0, keepdims=True)
    scale_down = lax.rsqrt(jnp.sum(diagonal, axis=1, keepdims=True))
    scale_across = lax.rsqrt(norms)
    unit = gram * scale_down * scale_across
    eye = jnp.where(row == col, 1.0, 0.0)
    keep = jnp.where(row > col, 1.0, jnp.where(row == col, 0.5, 0.0))
    unit_parts = halves(unit)
    inverse[...] = eye - (unit - eye) * keep

    def improve():
        now = inverse[...]
        parts = halves(now)
        moved = product(parts, unit_parts, PLAIN)
        excess = product(halves(moved), parts, OUTER) - eye
        inverse[...] = now - product(halves(excess * keep), parts, PLAIN)
        return jnp.sum(excess * excess)

    improve()
    _, error = lax.while_loop(
        lambda state: jnp.logical_and(state[0] < STEPS, jnp.logical_not(state[1] < CLOSE)),
        lambda state: (state[0] + 1, improve()),
        (2, improve()),
    )
    parts = halves(inverse[...])
    upper = product(parts, unit_parts, PLAIN) / scale_across
    upper_ref[...] = jnp.where(row <= col, upper, 0.0)
    matrix = matrix_ref[...] * scale_across
    basis_ref[...] = product(halves(matrix), parts, OUTER) * math.sqrt(D)
    done = jnp.logical_and(error < CLOSE, jnp.min(norms) > FLOOR)
    done_ref[0] = jnp.where(done, 1, 0)


def factor(packed, matrix):
    whole = jax.ShapeDtypeStruct(matrix.shape, F32)
    vmem = pl.BlockSpec(memory_space=pltpu.VMEM)
    return pl.pallas_call(
        factor_kernel,
        out_shape=(whole, whole, jax.ShapeDtypeStruct((1,), jnp.int32)),
        in_specs=[vmem, vmem],
        out_specs=(vmem, vmem, pl.BlockSpec(memory_space=pltpu.SMEM)),
        scratch_shapes=[pltpu.VMEM(matrix.shape, F32)],
        compiler_params=pltpu.CompilerParams(vmem_limit_bytes=32 * 1024 * 1024),
        name="factor",
    )(packed, matrix)


def orthonormal(matrix):
    local_gram = jnp.dot(matrix.T, matrix, precision=lax.Precision.HIGHEST)
    gram_total = total(local_gram, "feat")
    lower = jnp.linalg.cholesky(gram_total)
    solved = jax.scipy.linalg.solve_triangular(lower, matrix.T, lower=True)
    return (solved.T, lower.T)


def general(data, block_counts, basis):
    rows, rank = data.shape[0], basis.shape[1]
    active = lax.dynamic_index_in_dim(block_counts, lax.axis_index("dp"), 0, False)
    valid = lax.broadcasted_iota(jnp.int32, (rows, 1), 0) < active * BLOCK
    partial = jnp.dot(data, basis, preferred_element_type=F32)
    images = total(jnp.where(valid, partial, 0.0), "feat").astype(BF16)
    terms = lax.dot_general(
        data, images, (((0,), (0,)), ((), ())), preferred_element_type=F32
    )
    row_total = (jnp.sum(block_counts) * BLOCK).astype(F32)
    updated = basis.astype(F32) + total(terms, "dp") / row_total
    first_basis, upper_one = orthonormal(updated)
    second_basis, upper_two = orthonormal(first_basis)
    upper = jnp.dot(upper_two, upper_one, precision=lax.Precision.HIGHEST)
    return (second_basis * math.sqrt(D), upper)


def on_device(data, block_counts, basis):
    rows, columns = data.shape
    rank = basis.shape[1]
    dp = lax.axis_index("dp")
    feat = lax.axis_index("feat")
    dp_size = lax.axis_size("dp")
    core = feat % CORES
    here = rows // lax.axis_size("feat")
    active = lax.dynamic_index_in_dim(block_counts, dp, 0, False)
    row_ids = feat * here + lax.broadcasted_iota(jnp.int32, (here, 1), 0)
    valid = jnp.where(row_ids < active * BLOCK, 1.0, 0.0)
    row_total = (jnp.sum(block_counts) * BLOCK).astype(F32)
    beside = (valid, row_total, jnp.stack([dp % X, core]))
    images, beside = sum_images(data, basis, core, beside)
    valid, row_total, place = beside
    images = (images * valid).astype(F16)
    images = lax.all_gather(images, "feat", tiled=True).astype(BF16)

    terms = lax.dot_general(
        data, images, (((0,), (0,)), ((), ())), preferred_element_type=F32
    )
    terms = (terms / row_total).astype(F16)
    pieces = lax.all_to_all(terms.reshape(dp_size, columns // dp_size, rank), "dp", 0, 0)
    piece = jnp.sum(pieces.astype(F32), axis=0) / LIFT
    step = spread(piece, "dp", None, dp_size).reshape(columns, rank)
    updated, mine, theirs = gram_share(place, step, basis)
    basis_scaled, upper, done = factor(sum_gram(mine, theirs), updated)
    return lax.cond(
        done[0] == 1,
        lambda: (basis_scaled, upper),
        lambda: general(data, block_counts, basis),
    )


def solution(mesh):
    in_specs = (P("dp", "feat"), P(), P("feat", None))
    out_specs = (P("feat", None), P())
    return jax.shard_map(
        on_device, mesh=mesh, in_specs=in_specs, out_specs=out_specs, check_vma=False
    )
```

```python
import functools
import math

import jax
import jax.numpy as jnp
from jax import lax
from jax.experimental import pallas as pl
from jax.experimental.pallas import tpu as pltpu
from jax.sharding import PartitionSpec as P

D = 4096
BLOCK = 512
CORES = 2
X = 4
F32 = jnp.float32
BF16 = jnp.bfloat16
F16 = jnp.float16

LIFT = 16.0
TERMS = 32768.0
LIFT_STEP = 4.0
FLOOR = 1e-4
CLOSE = 4e-6
STEPS = 14

PLAIN = (((1,), (0,)), ((), ()))
ROWS = (((0,), (0,)), ((), ()))
OUTER = (((1,), (1,)), ((), ()))


def core_swap(value):
    count = lax.axis_size("feat")
    return lax.ppermute(value, "feat", [(i, i ^ 1) for i in range(count)])


def groups_z():
    count = lax.axis_size("feat")
    return [list(range(c, count, CORES)) for c in range(CORES)]


def groups_xc():
    count, width = lax.axis_size("dp"), lax.axis_size("feat")
    return [
        [(y + x) * width + z + c for x in range(X) for c in range(CORES)]
        for y in range(0, count, X)
        for z in range(0, width, CORES)
    ]


def spread(value, axis, groups, size):
    copies = jnp.broadcast_to(value[None], (size,) + value.shape)
    return lax.all_to_all(copies, axis, 0, 0, axis_index_groups=groups)


def total(value, axis):
    size = lax.axis_size(axis)
    pieces = lax.all_to_all(
        value.reshape((size, value.shape[0] // size) + value.shape[1:]), axis, 0, 0
    )
    return spread(jnp.sum(pieces, axis=0), axis, None, size).reshape(value.shape)


def sum_images(data, basis, core, beside):
    chips = lax.axis_size("feat") // CORES
    rows, columns = data.shape
    here = rows // (chips * CORES)
    split = data.reshape(chips, CORES, here, columns)

    def half(which):
        return lax.dynamic_index_in_dim(split, which, 1, False)

    def times(left, right):
        return lax.dot_general(
            left, right, (((2,), (0,)), ((), ())), preferred_element_type=F32
        )

    theirs = core_swap(
        jnp.concatenate([half(1 - core).reshape(chips * here, columns), basis])
    )
    mine, theirs, beside = lax.optimization_barrier(
        (times(half(core), basis), theirs, beside)
    )
    rows_there = theirs[: chips * here].reshape(chips, here, columns)
    pair = mine + times(rows_there, theirs[chips * here :])
    pieces = lax.all_to_all(
        (pair * LIFT).astype(F16), "feat", 0, 0, axis_index_groups=groups_z()
    )
    return jnp.sum(pieces.astype(F32), axis=0), beside


def gram_kernel(
    place_ref, counts_ref, step_ref, basis_ref, updated_ref, mine_ref, theirs_ref, packed
):
    count = counts_ref[0]
    for i in range(1, counts_ref.shape[0]):
        count += counts_ref[i]
    row_total = jnp.full((1, 1), count * BLOCK, jnp.int32).astype(F32)
    updated = basis_ref[...].astype(F32) + step_ref[...] * (TERMS / LIFT_STEP) / row_total
    updated_ref[...] = updated
    half = packed.shape[0]
    share = mine_ref.shape[0]
    dot = functools.partial(
        lax.dot_general,
        dimension_numbers=ROWS,
        precision=lax.Precision.HIGHEST,
        preferred_element_type=F32,
    )
    packed[:, : 2 * half] = dot(updated[:, :half], updated)
    packed[:, 2 * half :] = dot(updated[:, half:], updated[:, half:])
    first = place_ref[0] * CORES
    mine = pl.multiple_of((first + place_ref[1]) * share, share)
    theirs = pl.multiple_of((first + 1 - place_ref[1]) * share, share)
    mine_ref[...] = packed[pl.ds(mine, share), :]
    theirs_ref[...] = packed[pl.ds(theirs, share), :]


def gram_share(place, counts, step, basis):
    rank = basis.shape[1]
    half = rank // 2
    share = jax.ShapeDtypeStruct((half // (X * CORES), rank + half), F32)
    vmem = pl.BlockSpec(memory_space=pltpu.VMEM)
    smem = pl.BlockSpec(memory_space=pltpu.SMEM)
    return pl.pallas_call(
        gram_kernel,
        out_shape=(jax.ShapeDtypeStruct(basis.shape, F32), share, share),
        in_specs=[smem, smem, vmem, vmem],
        out_specs=(vmem, vmem, vmem),
        scratch_shapes=[pltpu.VMEM((half, rank + half), F32)],
        compiler_params=pltpu.CompilerParams(vmem_limit_bytes=32 * 1024 * 1024),
        name="gram_share",
    )(place, counts, step, basis)


def sum_gram(mine, theirs):
    chips = lax.axis_size("feat") // CORES
    pair = mine + core_swap(theirs)
    summed = jnp.sum(spread(pair, "feat", groups_z(), chips), axis=0)
    shares = spread(summed, ("dp", "feat"), groups_xc(), X * CORES)
    return shares.reshape(-1, shares.shape[-1])


def halves(value):
    high = value.astype(BF16)
    return high, (value - high.astype(F32)).astype(BF16)


def product(left, right, dims):
    dot = functools.partial(
        lax.dot_general, dimension_numbers=dims, preferred_element_type=F32
    )
    return dot(left[0], right[0]) + (dot(left[0], right[1]) + dot(left[1], right[0]))


def coarse(left, right, dims):
    return lax.dot_general(left[0], right[0], dims, preferred_element_type=F32)


def factor_kernel(packed_ref, matrix_ref, basis_ref, upper_ref, done_ref, inverse):
    half = packed_ref.shape[0]
    inverse[:half, :] = packed_ref[:, : 2 * half]
    inverse[half:, :half] = packed_ref[:, half : 2 * half].T
    inverse[half:, half:] = packed_ref[:, 2 * half :]
    gram = inverse[...]
    row = lax.broadcasted_iota(jnp.int32, gram.shape, 0)
    col = lax.broadcasted_iota(jnp.int32, gram.shape, 1)
    diagonal = jnp.where(row == col, gram, 0.0)
    norms = jnp.sum(diagonal, axis=0, keepdims=True)
    scale_down = lax.rsqrt(jnp.sum(diagonal, axis=1, keepdims=True))
    scale_across = lax.rsqrt(norms)
    unit = gram * scale_down * scale_across
    eye = jnp.where(row == col, 1.0, 0.0)
    keep = jnp.where(row > col, 1.0, jnp.where(row == col, 0.5, 0.0))
    unit_parts = halves(unit)
    inverse[...] = eye - (unit - eye) * keep

    def improve(multiply=product):
        now = inverse[...]
        parts = halves(now)
        moved = multiply(parts, unit_parts, PLAIN)
        excess = multiply(halves(moved), parts, OUTER) - eye
        inverse[...] = now - multiply(halves(excess * keep), parts, PLAIN)
        return jnp.sum(excess * excess)

    improve(coarse)
    _, error = lax.while_loop(
        lambda state: jnp.logical_and(state[0] < STEPS, jnp.logical_not(state[1] < CLOSE)),
        lambda state: (state[0] + 1, improve()),
        (2, improve()),
    )
    parts = halves(inverse[...])
    upper = product(parts, unit_parts, PLAIN) / scale_across
    upper_ref[...] = jnp.where(row <= col, upper, 0.0)
    matrix = matrix_ref[...] * scale_across
    basis_ref[...] = product(halves(matrix), parts, OUTER) * math.sqrt(D)
    done = jnp.logical_and(error < CLOSE, jnp.min(norms) > FLOOR)
    done_ref[0] = jnp.where(done, 1, 0)


def factor(packed, matrix):
    whole = jax.ShapeDtypeStruct(matrix.shape, F32)
    vmem = pl.BlockSpec(memory_space=pltpu.VMEM)
    return pl.pallas_call(
        factor_kernel,
        out_shape=(whole, whole, jax.ShapeDtypeStruct((1,), jnp.int32)),
        in_specs=[vmem, vmem],
        out_specs=(vmem, vmem, pl.BlockSpec(memory_space=pltpu.SMEM)),
        scratch_shapes=[pltpu.VMEM(matrix.shape, F32)],
        compiler_params=pltpu.CompilerParams(vmem_limit_bytes=32 * 1024 * 1024),
        name="factor",
    )(packed, matrix)


def orthonormal(matrix):
    local_gram = jnp.dot(matrix.T, matrix, precision=lax.Precision.HIGHEST)
    gram_total = total(local_gram, "feat")
    lower = jnp.linalg.cholesky(gram_total)
    solved = jax.scipy.linalg.solve_triangular(lower, matrix.T, lower=True)
    return (solved.T, lower.T)


def general(data, block_counts, basis):
    rows, rank = data.shape[0], basis.shape[1]
    active = lax.dynamic_index_in_dim(block_counts, lax.axis_index("dp"), 0, False)
    valid = lax.broadcasted_iota(jnp.int32, (rows, 1), 0) < active * BLOCK
    partial = jnp.dot(data, basis, preferred_element_type=F32)
    images = total(jnp.where(valid, partial, 0.0), "feat").astype(BF16)
    terms = lax.dot_general(
        data, images, (((0,), (0,)), ((), ())), preferred_element_type=F32
    )
    row_total = (jnp.sum(block_counts) * BLOCK).astype(F32)
    updated = basis.astype(F32) + total(terms, "dp") / row_total
    first_basis, upper_one = orthonormal(updated)
    second_basis, upper_two = orthonormal(first_basis)
    upper = jnp.dot(upper_two, upper_one, precision=lax.Precision.HIGHEST)
    return (second_basis * math.sqrt(D), upper)


def on_device(data, block_counts, basis):
    rows, columns = data.shape
    rank = basis.shape[1]
    dp = lax.axis_index("dp")
    feat = lax.axis_index("feat")
    dp_size = lax.axis_size("dp")
    core = feat % CORES
    here = rows // lax.axis_size("feat")
    active = lax.dynamic_index_in_dim(block_counts, dp, 0, False)
    row_ids = feat * here + lax.broadcasted_iota(jnp.int32, (here, 1), 0)
    valid = jnp.where(row_ids < active * BLOCK, 1.0, 0.0)
    beside = (valid, jnp.stack([dp % X, core]))
    images, beside = sum_images(data, basis, core, beside)
    valid, place = beside
    images = lax.reduce_precision(images * valid, 8, 7).astype(F16)
    images = lax.all_gather(images, "feat", tiled=True).astype(BF16)

    terms = lax.dot_general(
        data, images, (((0,), (0,)), ((), ())), preferred_element_type=F32
    )
    terms = (terms / TERMS).astype(F16)
    pieces = lax.all_to_all(terms.reshape(dp_size, columns // dp_size, rank), "dp", 0, 0)
    piece = (jnp.sum(pieces.astype(F32), axis=0) * (LIFT_STEP / LIFT)).astype(F16)
    step = spread(piece, "dp", None, dp_size).reshape(columns, rank).astype(F32)
    updated, mine, theirs = gram_share(place, block_counts, step, basis)
    basis_scaled, upper, done = factor(sum_gram(mine, theirs), updated)
    return lax.cond(
        done[0] == 1,
        lambda: (basis_scaled, upper),
        lambda: general(data, block_counts, basis),
    )


def solution(mesh):
    in_specs = (P("dp", "feat"), P(), P("feat", None))
    out_specs = (P("feat", None), P())
    return jax.shard_map(
        on_device, mesh=mesh, in_specs=in_specs, out_specs=out_specs, check_vma=False
    )
```

```python
import functools
import math

import jax
import jax.numpy as jnp
from jax import lax
from jax.experimental import pallas as pl
from jax.experimental.pallas import tpu as pltpu
from jax.sharding import PartitionSpec as P

D = 4096
BLOCK = 512
CORES = 2
X = 4
F32 = jnp.float32
BF16 = jnp.bfloat16
F16 = jnp.float16

LIFT = 16.0
TERMS = 32768.0
LIFT_STEP = 4.0
FLOOR = 1e-4
CLOSE = 4e-6
STEPS = 14

PLAIN = (((1,), (0,)), ((), ()))
ROWS = (((0,), (0,)), ((), ()))
OUTER = (((1,), (1,)), ((), ()))


def core_swap(value):
    count = lax.axis_size("feat")
    return lax.ppermute(value, "feat", [(i, i ^ 1) for i in range(count)])


def groups_z():
    count = lax.axis_size("feat")
    return [list(range(c, count, CORES)) for c in range(CORES)]


def groups_xc():
    count, width = lax.axis_size("dp"), lax.axis_size("feat")
    return [
        [(y + x) * width + z + c for x in range(X) for c in range(CORES)]
        for y in range(0, count, X)
        for z in range(0, width, CORES)
    ]


def spread(value, axis, groups, size):
    copies = jnp.broadcast_to(value[None], (size,) + value.shape)
    return lax.all_to_all(copies, axis, 0, 0, axis_index_groups=groups)


def total(value, axis):
    size = lax.axis_size(axis)
    pieces = lax.all_to_all(
        value.reshape((size, value.shape[0] // size) + value.shape[1:]), axis, 0, 0
    )
    return spread(jnp.sum(pieces, axis=0), axis, None, size).reshape(value.shape)


def sum_images(data, basis, core, beside):
    chips = lax.axis_size("feat") // CORES
    rows, columns = data.shape
    here = rows // (chips * CORES)
    split = data.reshape(chips, CORES, here, columns)

    def half(which):
        return lax.dynamic_index_in_dim(split, which, 1, False)

    def times(left, right):
        return lax.dot_general(
            left, right, (((2,), (0,)), ((), ())), preferred_element_type=F32
        )

    whole = times(split.reshape(chips, CORES * here, columns), basis)
    whole = whole.reshape(chips, CORES, here, -1)
    theirs = core_swap(
        (lax.dynamic_index_in_dim(whole, 1 - core, 1, False) * LIFT).astype(F16)
    )
    mine, theirs, beside = lax.optimization_barrier(
        (lax.dynamic_index_in_dim(whole, core, 1, False), theirs, beside)
    )
    pair = mine + theirs.astype(F32) / LIFT
    pieces = lax.all_to_all(
        (pair * LIFT).astype(F16), "feat", 0, 0, axis_index_groups=groups_z()
    )
    return jnp.sum(pieces.astype(F32), axis=0), beside


def gram_kernel(
    place_ref, counts_ref, step_ref, basis_ref, updated_ref, mine_ref, theirs_ref, packed
):
    count = counts_ref[0]
    for i in range(1, counts_ref.shape[0]):
        count += counts_ref[i]
    row_total = jnp.full((1, 1), count * BLOCK, jnp.int32).astype(F32)
    updated = basis_ref[...].astype(F32) + step_ref[...] * (TERMS / LIFT_STEP) / row_total
    updated_ref[...] = updated
    half = packed.shape[0]
    share = mine_ref.shape[0]
    dot = functools.partial(
        lax.dot_general,
        dimension_numbers=ROWS,
        precision=lax.Precision.HIGHEST,
        preferred_element_type=F32,
    )
    packed[:, : 2 * half] = dot(updated[:, :half], updated)
    packed[:, 2 * half :] = dot(updated[:, half:], updated[:, half:])
    first = place_ref[0] * CORES
    mine = pl.multiple_of((first + place_ref[1]) * share, share)
    theirs = pl.multiple_of((first + 1 - place_ref[1]) * share, share)
    mine_ref[...] = packed[pl.ds(mine, share), :]
    theirs_ref[...] = packed[pl.ds(theirs, share), :]


def gram_share(place, counts, step, basis):
    rank = basis.shape[1]
    half = rank // 2
    share = jax.ShapeDtypeStruct((half // (X * CORES), rank + half), F32)
    vmem = pl.BlockSpec(memory_space=pltpu.VMEM)
    smem = pl.BlockSpec(memory_space=pltpu.SMEM)
    return pl.pallas_call(
        gram_kernel,
        out_shape=(jax.ShapeDtypeStruct(basis.shape, F32), share, share),
        in_specs=[smem, smem, vmem, vmem],
        out_specs=(vmem, vmem, vmem),
        scratch_shapes=[pltpu.VMEM((half, rank + half), F32)],
        compiler_params=pltpu.CompilerParams(vmem_limit_bytes=32 * 1024 * 1024),
        name="gram_share",
    )(place, counts, step, basis)


def sum_gram(mine, theirs):
    chips = lax.axis_size("feat") // CORES
    pair = mine + core_swap(theirs)
    summed = jnp.sum(spread(pair, "feat", groups_z(), chips), axis=0)
    shares = spread(summed, ("dp", "feat"), groups_xc(), X * CORES)
    return shares.reshape(-1, shares.shape[-1])


def halves(value):
    high = value.astype(BF16)
    return high, (value - high.astype(F32)).astype(BF16)


def product(left, right, dims):
    dot = functools.partial(
        lax.dot_general, dimension_numbers=dims, preferred_element_type=F32
    )
    return dot(left[0], right[0]) + (dot(left[0], right[1]) + dot(left[1], right[0]))


def coarse(left, right, dims):
    return lax.dot_general(left[0], right[0], dims, preferred_element_type=F32)


def factor_kernel(packed_ref, matrix_ref, basis_ref, upper_ref, done_ref, inverse):
    half = packed_ref.shape[0]
    inverse[:half, :] = packed_ref[:, : 2 * half]
    inverse[half:, :half] = packed_ref[:, half : 2 * half].T
    inverse[half:, half:] = packed_ref[:, 2 * half :]
    gram = inverse[...]
    row = lax.broadcasted_iota(jnp.int32, gram.shape, 0)
    col = lax.broadcasted_iota(jnp.int32, gram.shape, 1)
    diagonal = jnp.where(row == col, gram, 0.0)
    norms = jnp.sum(diagonal, axis=0, keepdims=True)
    scale_down = lax.rsqrt(jnp.sum(diagonal, axis=1, keepdims=True))
    scale_across = lax.rsqrt(norms)
    unit = gram * scale_down * scale_across
    eye = jnp.where(row == col, 1.0, 0.0)
    keep = jnp.where(row > col, 1.0, jnp.where(row == col, 0.5, 0.0))
    unit_parts = halves(unit)
    inverse[...] = eye - (unit - eye) * keep

    def improve(multiply=product):
        now = inverse[...]
        parts = halves(now)
        moved = multiply(parts, unit_parts, PLAIN)
        excess = multiply(halves(moved), parts, OUTER) - eye
        inverse[...] = now - multiply(halves(excess * keep), parts, PLAIN)
        return jnp.sum(excess * excess)

    improve(coarse)
    _, error = lax.while_loop(
        lambda state: jnp.logical_and(state[0] < STEPS, jnp.logical_not(state[1] < CLOSE)),
        lambda state: (state[0] + 1, improve()),
        (2, improve()),
    )
    parts = halves(inverse[...])
    upper = product(parts, unit_parts, PLAIN) / scale_across
    upper_ref[...] = jnp.where(row <= col, upper, 0.0)
    matrix = matrix_ref[...] * scale_across
    basis_ref[...] = product(halves(matrix), parts, OUTER) * math.sqrt(D)
    done = jnp.logical_and(error < CLOSE, jnp.min(norms) > FLOOR)
    done_ref[0] = jnp.where(done, 1, 0)


def factor(packed, matrix):
    whole = jax.ShapeDtypeStruct(matrix.shape, F32)
    vmem = pl.BlockSpec(memory_space=pltpu.VMEM)
    return pl.pallas_call(
        factor_kernel,
        out_shape=(whole, whole, jax.ShapeDtypeStruct((1,), jnp.int32)),
        in_specs=[vmem, vmem],
        out_specs=(vmem, vmem, pl.BlockSpec(memory_space=pltpu.SMEM)),
        scratch_shapes=[pltpu.VMEM(matrix.shape, F32)],
        compiler_params=pltpu.CompilerParams(vmem_limit_bytes=32 * 1024 * 1024),
        name="factor",
    )(packed, matrix)


def orthonormal(matrix):
    local_gram = jnp.dot(matrix.T, matrix, precision=lax.Precision.HIGHEST)
    gram_total = total(local_gram, "feat")
    lower = jnp.linalg.cholesky(gram_total)
    solved = jax.scipy.linalg.solve_triangular(lower, matrix.T, lower=True)
    return (solved.T, lower.T)


def general(data, block_counts, basis):
    rows, rank = data.shape[0], basis.shape[1]
    active = lax.dynamic_index_in_dim(block_counts, lax.axis_index("dp"), 0, False)
    valid = lax.broadcasted_iota(jnp.int32, (rows, 1), 0) < active * BLOCK
    partial = jnp.dot(data, basis, preferred_element_type=F32)
    images = total(jnp.where(valid, partial, 0.0), "feat").astype(BF16)
    terms = lax.dot_general(
        data, images, (((0,), (0,)), ((), ())), preferred_element_type=F32
    )
    row_total = (jnp.sum(block_counts) * BLOCK).astype(F32)
    updated = basis.astype(F32) + total(terms, "dp") / row_total
    first_basis, upper_one = orthonormal(updated)
    second_basis, upper_two = orthonormal(first_basis)
    upper = jnp.dot(upper_two, upper_one, precision=lax.Precision.HIGHEST)
    return (second_basis * math.sqrt(D), upper)


def on_device(data, block_counts, basis):
    rows, columns = data.shape
    rank = basis.shape[1]
    dp = lax.axis_index("dp")
    feat = lax.axis_index("feat")
    dp_size = lax.axis_size("dp")
    core = feat % CORES
    here = rows // lax.axis_size("feat")
    active = lax.dynamic_index_in_dim(block_counts, dp, 0, False)
    row_ids = feat * here + lax.broadcasted_iota(jnp.int32, (here, 1), 0)
    valid = jnp.where(row_ids < active * BLOCK, 1.0, 0.0)
    beside = (valid, jnp.stack([dp % X, core]))
    images, beside = sum_images(data, basis, core, beside)
    valid, place = beside
    images = lax.reduce_precision(images * valid, 8, 7).astype(F16)
    images = lax.all_gather(images, "feat", tiled=True).astype(BF16)

    terms = lax.dot_general(
        data, images, (((0,), (0,)), ((), ())), preferred_element_type=F32
    )
    terms = (terms / TERMS).astype(F16)
    pieces = lax.all_to_all(terms.reshape(dp_size, columns // dp_size, rank), "dp", 0, 0)
    piece = (jnp.sum(pieces.astype(F32), axis=0) * (LIFT_STEP / LIFT)).astype(F16)
    step = spread(piece, "dp", None, dp_size).reshape(columns, rank).astype(F32)
    updated, mine, theirs = gram_share(place, block_counts, step, basis)
    gram, data, block_counts, basis = lax.optimization_barrier(
        (sum_gram(mine, theirs), data, block_counts, basis)
    )
    basis_scaled, upper, done = factor(gram, updated)
    return lax.cond(
        done[0] == 1,
        lambda: (basis_scaled, upper),
        lambda: general(data, block_counts, basis),
    )


def solution(mesh):
    in_specs = (P("dp", "feat"), P(), P("feat", None))
    out_specs = (P("feat", None), P())
    return jax.shard_map(
        on_device, mesh=mesh, in_specs=in_specs, out_specs=out_specs, check_vma=False
    )
```

```python
import functools
import math

import jax
import jax.numpy as jnp
from jax import lax
from jax.experimental import pallas as pl
from jax.experimental.pallas import tpu as pltpu
from jax.sharding import PartitionSpec as P

D = 4096
BLOCK = 512
CORES = 2
X = 4
F32 = jnp.float32
BF16 = jnp.bfloat16
F16 = jnp.float16

LIFT = 16.0
TERMS = 32768.0
LIFT_STEP = 4.0
FLOOR = 1e-4
CLOSE = 4e-6
STEPS = 14

PLAIN = (((1,), (0,)), ((), ()))
ROWS = (((0,), (0,)), ((), ()))
OUTER = (((1,), (1,)), ((), ()))


def core_swap(value):
    count = lax.axis_size("feat")
    return lax.ppermute(value, "feat", [(i, i ^ 1) for i in range(count)])


def groups_z():
    count = lax.axis_size("feat")
    return [list(range(c, count, CORES)) for c in range(CORES)]


def groups_xc():
    count, width = lax.axis_size("dp"), lax.axis_size("feat")
    return [
        [(y + x) * width + z + c for x in range(X) for c in range(CORES)]
        for y in range(0, count, X)
        for z in range(0, width, CORES)
    ]


def spread(value, axis, groups, size):
    copies = jnp.broadcast_to(value[None], (size,) + value.shape)
    return lax.all_to_all(copies, axis, 0, 0, axis_index_groups=groups)


def total(value, axis):
    size = lax.axis_size(axis)
    pieces = lax.all_to_all(
        value.reshape((size, value.shape[0] // size) + value.shape[1:]), axis, 0, 0
    )
    return spread(jnp.sum(pieces, axis=0), axis, None, size).reshape(value.shape)


def half_images(data, basis, active, core):
    half = data.shape[0] // CORES
    whole = jnp.dot(data, basis, preferred_element_type=F32).reshape(CORES, half, -1)
    theirs = core_swap(
        (lax.dynamic_index_in_dim(whole, 1 - core, 0, False) * LIFT).astype(F16)
    )
    row_ids = core * half + lax.broadcasted_iota(jnp.int32, (half, 1), 0)
    valid = jnp.where(row_ids < active * BLOCK, 1.0, 0.0)
    mine, theirs, valid = lax.optimization_barrier(
        (lax.dynamic_index_in_dim(whole, core, 0, False) * LIFT, theirs, valid)
    )
    pair = ((mine + theirs.astype(F32)) * valid).astype(F16)
    return lax.psum(pair, "feat", axis_index_groups=groups_z())


def column_terms(data, basis, active, core):
    half = data.shape[0] // CORES
    split = data.reshape(CORES, half, -1)

    def terms(which, images):
        rows = lax.dynamic_index_in_dim(split, which, 0, False)
        return lax.dot_general(
            rows, images.astype(BF16), ROWS, preferred_element_type=F32
        )

    images = half_images(data, basis, active, core)
    own, theirs = lax.optimization_barrier((terms(core, images), core_swap(images)))
    return ((own + terms(1 - core, theirs)) / TERMS).astype(F16)


def gram_kernel(counts_ref, step_ref, basis_ref, updated_ref, mine_ref, theirs_ref, packed):
    count = counts_ref[0]
    for i in range(1, counts_ref.shape[0]):
        count += counts_ref[i]
    row_total = jnp.full((1, 1), count * BLOCK, jnp.int32).astype(F32)
    updated = basis_ref[...].astype(F32) + step_ref[...] * (TERMS / LIFT_STEP) / row_total
    updated_ref[...] = updated
    half = packed.shape[0]
    share = mine_ref.shape[0]
    dot = functools.partial(
        lax.dot_general,
        dimension_numbers=ROWS,
        precision=lax.Precision.HIGHEST,
        preferred_element_type=F32,
    )
    packed[:, : 2 * half] = dot(updated[:, :half], updated)
    packed[:, 2 * half :] = dot(updated[:, half:], updated[:, half:])
    first = lax.rem(lax.axis_index("dp"), X) * CORES
    core = lax.rem(lax.axis_index("feat"), CORES)
    mine = pl.multiple_of((first + core) * share, share)
    theirs = pl.multiple_of((first + 1 - core) * share, share)
    mine_ref[...] = packed[pl.ds(mine, share), :]
    theirs_ref[...] = packed[pl.ds(theirs, share), :]


def gram_share(counts, step, basis):
    rank = basis.shape[1]
    half = rank // 2
    share = jax.ShapeDtypeStruct((half // (X * CORES), rank + half), F32)
    vmem = pl.BlockSpec(memory_space=pltpu.VMEM)
    smem = pl.BlockSpec(memory_space=pltpu.SMEM)
    return pl.pallas_call(
        gram_kernel,
        out_shape=(jax.ShapeDtypeStruct(basis.shape, F32), share, share),
        in_specs=[smem, vmem, vmem],
        out_specs=(vmem, vmem, vmem),
        scratch_shapes=[pltpu.VMEM((half, rank + half), F32)],
        compiler_params=pltpu.CompilerParams(vmem_limit_bytes=32 * 1024 * 1024),
        name="gram_share",
    )(counts, step, basis)


def sum_gram(mine, theirs):
    chips = lax.axis_size("feat") // CORES
    pair = mine + core_swap(theirs)
    summed = jnp.sum(spread(pair, "feat", groups_z(), chips), axis=0)
    shares = spread(summed, ("dp", "feat"), groups_xc(), X * CORES)
    return shares.reshape(-1, shares.shape[-1])


def halves(value):
    high = value.astype(BF16)
    return high, (value - high.astype(F32)).astype(BF16)


def product(left, right, dims):
    dot = functools.partial(
        lax.dot_general, dimension_numbers=dims, preferred_element_type=F32
    )
    return dot(left[0], right[0]) + (dot(left[0], right[1]) + dot(left[1], right[0]))


def coarse(left, right, dims):
    return lax.dot_general(left[0], right[0], dims, preferred_element_type=F32)


def factor_kernel(packed_ref, matrix_ref, basis_ref, upper_ref, done_ref, inverse):
    half = packed_ref.shape[0]
    inverse[:half, :] = packed_ref[:, : 2 * half]
    inverse[half:, :half] = packed_ref[:, half : 2 * half].T
    inverse[half:, half:] = packed_ref[:, 2 * half :]
    gram = inverse[...]
    row = lax.broadcasted_iota(jnp.int32, gram.shape, 0)
    col = lax.broadcasted_iota(jnp.int32, gram.shape, 1)
    diagonal = jnp.where(row == col, gram, 0.0)
    norms = jnp.sum(diagonal, axis=0, keepdims=True)
    scale_down = lax.rsqrt(jnp.sum(diagonal, axis=1, keepdims=True))
    scale_across = lax.rsqrt(norms)
    unit = gram * scale_down * scale_across
    eye = jnp.where(row == col, 1.0, 0.0)
    keep = jnp.where(row > col, 1.0, jnp.where(row == col, 0.5, 0.0))
    unit_parts = halves(unit)
    inverse[...] = eye - (unit - eye) * keep

    def improve(multiply=product):
        now = inverse[...]
        parts = halves(now)
        moved = multiply(parts, unit_parts, PLAIN)
        excess = multiply(halves(moved), parts, OUTER) - eye
        inverse[...] = now - coarse(halves(excess * keep), parts, PLAIN)
        return jnp.sum(excess * excess)

    improve(coarse)
    _, error = lax.while_loop(
        lambda state: jnp.logical_and(state[0] < STEPS, jnp.logical_not(state[1] < CLOSE)),
        lambda state: (state[0] + 1, improve()),
        (2, improve()),
    )
    parts = halves(inverse[...])
    upper = product(parts, unit_parts, PLAIN) / scale_across
    upper_ref[...] = jnp.where(row <= col, upper, 0.0)
    matrix = matrix_ref[...] * scale_across
    basis_ref[...] = product(halves(matrix), parts, OUTER) * math.sqrt(D)
    done = jnp.logical_and(error < CLOSE, jnp.min(norms) > FLOOR)
    done_ref[0] = jnp.where(done, 1, 0)


def factor(packed, matrix):
    whole = jax.ShapeDtypeStruct(matrix.shape, F32)
    vmem = pl.BlockSpec(memory_space=pltpu.VMEM)
    return pl.pallas_call(
        factor_kernel,
        out_shape=(whole, whole, jax.ShapeDtypeStruct((1,), jnp.int32)),
        in_specs=[vmem, vmem],
        out_specs=(vmem, vmem, pl.BlockSpec(memory_space=pltpu.SMEM)),
        scratch_shapes=[pltpu.VMEM(matrix.shape, F32)],
        compiler_params=pltpu.CompilerParams(vmem_limit_bytes=32 * 1024 * 1024),
        name="factor",
    )(packed, matrix)


def orthonormal(matrix):
    local_gram = jnp.dot(matrix.T, matrix, precision=lax.Precision.HIGHEST)
    gram_total = total(local_gram, "feat")
    lower = jnp.linalg.cholesky(gram_total)
    solved = jax.scipy.linalg.solve_triangular(lower, matrix.T, lower=True)
    return (solved.T, lower.T)


def general(data, block_counts, basis):
    rows, rank = data.shape[0], basis.shape[1]
    active = lax.dynamic_index_in_dim(block_counts, lax.axis_index("dp"), 0, False)
    valid = lax.broadcasted_iota(jnp.int32, (rows, 1), 0) < active * BLOCK
    partial = jnp.dot(data, basis, preferred_element_type=F32)
    images = total(jnp.where(valid, partial, 0.0), "feat").astype(BF16)
    terms = lax.dot_general(
        data, images, (((0,), (0,)), ((), ())), preferred_element_type=F32
    )
    row_total = (jnp.sum(block_counts) * BLOCK).astype(F32)
    updated = basis.astype(F32) + total(terms, "dp") / row_total
    first_basis, upper_one = orthonormal(updated)
    second_basis, upper_two = orthonormal(first_basis)
    upper = jnp.dot(upper_two, upper_one, precision=lax.Precision.HIGHEST)
    return (second_basis * math.sqrt(D), upper)


def on_device(data, block_counts, basis):
    rows, columns = data.shape
    rank = basis.shape[1]
    dp = lax.axis_index("dp")
    feat = lax.axis_index("feat")
    dp_size = lax.axis_size("dp")
    active = lax.dynamic_index_in_dim(block_counts, dp, 0, False)
    terms = column_terms(data, basis, active, feat % CORES)
    pieces = lax.all_to_all(terms.reshape(dp_size, columns // dp_size, rank), "dp", 0, 0)
    piece = (jnp.sum(pieces.astype(F32), axis=0) * (LIFT_STEP / LIFT)).astype(F16)
    step = spread(piece, "dp", None, dp_size).reshape(columns, rank).astype(F32)
    updated, mine, theirs = gram_share(block_counts, step, basis)
    gram, data, block_counts, basis = lax.optimization_barrier(
        (sum_gram(mine, theirs), data, block_counts, basis)
    )
    basis_scaled, upper, done = factor(gram, updated)
    return lax.cond(
        done[0] == 1,
        lambda: (basis_scaled, upper),
        lambda: general(data, block_counts, basis),
    )


def solution(mesh):
    in_specs = (P("dp", "feat"), P(), P("feat", None))
    out_specs = (P("feat", None), P())
    return jax.shard_map(
        on_device, mesh=mesh, in_specs=in_specs, out_specs=out_specs, check_vma=False
    )
```

```python
import functools
import math

import jax
import jax.numpy as jnp
from jax import lax
from jax.experimental import pallas as pl
from jax.experimental.pallas import tpu as pltpu
from jax.sharding import PartitionSpec as P

D = 4096
BLOCK = 512
CORES = 2
X = 4
ROW_PAIR = 2
F32 = jnp.float32
BF16 = jnp.bfloat16
F16 = jnp.float16

LIFT = 16.0
TERMS = 32768.0
LIFT_STEP = 4.0
FLOOR = 1e-4
CLOSE = 4e-6
STEPS = 14

PLAIN = (((1,), (0,)), ((), ()))
ROWS = (((0,), (0,)), ((), ()))
OUTER = (((1,), (1,)), ((), ()))


def core_swap(value):
    count = lax.axis_size("feat")
    return lax.ppermute(value, "feat", [(i, i ^ 1) for i in range(count)])


def groups_z():
    count = lax.axis_size("feat")
    return [list(range(c, count, CORES)) for c in range(CORES)]


def groups_near():
    count, width = lax.axis_size("dp"), lax.axis_size("feat")
    near = X * ROW_PAIR
    return [
        [(first + i) * width + z + c for i in range(near) for c in range(CORES)]
        for first in range(0, count, near)
        for z in range(0, width, CORES)
    ]


def spread(value, axis, groups, size):
    copies = jnp.broadcast_to(value[None], (size,) + value.shape)
    return lax.all_to_all(copies, axis, 0, 0, axis_index_groups=groups)


def total(value, axis):
    size = lax.axis_size(axis)
    pieces = lax.all_to_all(
        value.reshape((size, value.shape[0] // size) + value.shape[1:]), axis, 0, 0
    )
    return spread(jnp.sum(pieces, axis=0), axis, None, size).reshape(value.shape)


def half_images(data, basis, active, core):
    half = data.shape[0] // CORES
    whole = jnp.dot(data, basis, preferred_element_type=F32).reshape(CORES, half, -1)
    theirs = core_swap(
        (lax.dynamic_index_in_dim(whole, 1 - core, 0, False) * LIFT).astype(F16)
    )
    row_ids = core * half + lax.broadcasted_iota(jnp.int32, (half, 1), 0)
    valid = jnp.where(row_ids < active * BLOCK, 1.0, 0.0)
    mine, theirs, valid = lax.optimization_barrier(
        (lax.dynamic_index_in_dim(whole, core, 0, False) * LIFT, theirs, valid)
    )
    pair = ((mine + theirs.astype(F32)) * valid).astype(F16)
    return lax.psum(pair, "feat", axis_index_groups=groups_z())


def column_terms(data, basis, active, core):
    half = data.shape[0] // CORES
    split = data.reshape(CORES, half, -1)

    def terms(which, images):
        rows = lax.dynamic_index_in_dim(split, which, 0, False)
        return lax.dot_general(
            rows, images.astype(BF16), ROWS, preferred_element_type=F32
        )

    images = half_images(data, basis, active, core)
    own, theirs = lax.optimization_barrier((terms(core, images), core_swap(images)))
    return ((own + terms(1 - core, theirs)) / TERMS).astype(F16)


def gram_kernel(counts_ref, step_ref, basis_ref, updated_ref, mine_ref, theirs_ref, packed):
    count = counts_ref[0]
    for i in range(1, counts_ref.shape[0]):
        count += counts_ref[i]
    row_total = jnp.full((1, 1), count * BLOCK, jnp.int32).astype(F32)
    updated = basis_ref[...].astype(F32) + step_ref[...] * (TERMS / LIFT_STEP) / row_total
    updated_ref[...] = updated
    half = packed.shape[0]
    share = mine_ref.shape[0]
    dot = functools.partial(
        lax.dot_general,
        dimension_numbers=ROWS,
        precision=lax.Precision.HIGHEST,
        preferred_element_type=F32,
    )
    packed[:, : 2 * half] = dot(updated[:, :half], updated)
    packed[:, 2 * half :] = dot(updated[:, half:], updated[:, half:])
    first = lax.rem(lax.axis_index("dp"), X * ROW_PAIR) * CORES
    core = lax.rem(lax.axis_index("feat"), CORES)
    mine = pl.multiple_of((first + core) * share, share)
    theirs = pl.multiple_of((first + 1 - core) * share, share)
    mine_ref[...] = packed[pl.ds(mine, share), :]
    theirs_ref[...] = packed[pl.ds(theirs, share), :]


def gram_share(counts, step, basis):
    rank = basis.shape[1]
    half = rank // 2
    share = jax.ShapeDtypeStruct((half // (X * ROW_PAIR * CORES), rank + half), F32)
    vmem = pl.BlockSpec(memory_space=pltpu.VMEM)
    smem = pl.BlockSpec(memory_space=pltpu.SMEM)
    return pl.pallas_call(
        gram_kernel,
        out_shape=(jax.ShapeDtypeStruct(basis.shape, F32), share, share),
        in_specs=[smem, vmem, vmem],
        out_specs=(vmem, vmem, vmem),
        scratch_shapes=[pltpu.VMEM((half, rank + half), F32)],
        compiler_params=pltpu.CompilerParams(vmem_limit_bytes=32 * 1024 * 1024),
        name="gram_share",
    )(counts, step, basis)


def sum_gram(mine, theirs):
    chips = lax.axis_size("feat") // CORES
    pair = mine + core_swap(theirs)
    summed = jnp.sum(spread(pair, "feat", groups_z(), chips), axis=0)
    shares = spread(summed, ("dp", "feat"), groups_near(), X * ROW_PAIR * CORES)
    return shares.reshape(-1, shares.shape[-1])


def halves(value):
    high = value.astype(BF16)
    return high, (value - high.astype(F32)).astype(BF16)


def product(left, right, dims):
    dot = functools.partial(
        lax.dot_general, dimension_numbers=dims, preferred_element_type=F32
    )
    return dot(left[0], right[0]) + (dot(left[0], right[1]) + dot(left[1], right[0]))


def coarse(left, right, dims):
    return lax.dot_general(left[0], right[0], dims, preferred_element_type=F32)


def factor_kernel(packed_ref, matrix_ref, basis_ref, upper_ref, done_ref, inverse):
    half = packed_ref.shape[0]
    inverse[:half, :] = packed_ref[:, : 2 * half]
    inverse[half:, :half] = packed_ref[:, half : 2 * half].T
    inverse[half:, half:] = packed_ref[:, 2 * half :]
    gram = inverse[...]
    row = lax.broadcasted_iota(jnp.int32, gram.shape, 0)
    col = lax.broadcasted_iota(jnp.int32, gram.shape, 1)
    diagonal = jnp.where(row == col, gram, 0.0)
    norms = jnp.sum(diagonal, axis=0, keepdims=True)
    scale_down = lax.rsqrt(jnp.sum(diagonal, axis=1, keepdims=True))
    scale_across = lax.rsqrt(norms)
    unit = gram * scale_down * scale_across
    eye = jnp.where(row == col, 1.0, 0.0)
    keep = jnp.where(row > col, 1.0, jnp.where(row == col, 0.5, 0.0))
    unit_parts = halves(unit)
    inverse[...] = eye - (unit - eye) * keep

    def improve(multiply=product):
        now = inverse[...]
        parts = halves(now)
        moved = multiply(parts, unit_parts, PLAIN)
        excess = multiply(halves(moved), parts, OUTER) - eye
        inverse[...] = now - coarse(halves(excess * keep), parts, PLAIN)
        return jnp.sum(excess * excess)

    improve(coarse)
    _, error = lax.while_loop(
        lambda state: jnp.logical_and(state[0] < STEPS, jnp.logical_not(state[1] < CLOSE)),
        lambda state: (state[0] + 1, improve()),
        (2, improve()),
    )
    parts = halves(inverse[...])
    upper = product(parts, unit_parts, PLAIN) / scale_across
    upper_ref[...] = jnp.where(row <= col, upper, 0.0)
    matrix = matrix_ref[...] * scale_across
    basis_ref[...] = product(halves(matrix), parts, OUTER) * math.sqrt(D)
    done = jnp.logical_and(error < CLOSE, jnp.min(norms) > FLOOR)
    done_ref[0] = jnp.where(done, 1, 0)


def factor(packed, matrix):
    whole = jax.ShapeDtypeStruct(matrix.shape, F32)
    vmem = pl.BlockSpec(memory_space=pltpu.VMEM)
    return pl.pallas_call(
        factor_kernel,
        out_shape=(whole, whole, jax.ShapeDtypeStruct((1,), jnp.int32)),
        in_specs=[vmem, vmem],
        out_specs=(vmem, vmem, pl.BlockSpec(memory_space=pltpu.SMEM)),
        scratch_shapes=[pltpu.VMEM(matrix.shape, F32)],
        compiler_params=pltpu.CompilerParams(vmem_limit_bytes=32 * 1024 * 1024),
        name="factor",
    )(packed, matrix)


def orthonormal(matrix):
    local_gram = jnp.dot(matrix.T, matrix, precision=lax.Precision.HIGHEST)
    gram_total = total(local_gram, "feat")
    lower = jnp.linalg.cholesky(gram_total)
    solved = jax.scipy.linalg.solve_triangular(lower, matrix.T, lower=True)
    return (solved.T, lower.T)


def general(data, block_counts, basis):
    rows, rank = data.shape[0], basis.shape[1]
    active = lax.dynamic_index_in_dim(block_counts, lax.axis_index("dp"), 0, False)
    valid = lax.broadcasted_iota(jnp.int32, (rows, 1), 0) < active * BLOCK
    partial = jnp.dot(data, basis, preferred_element_type=F32)
    images = total(jnp.where(valid, partial, 0.0), "feat").astype(BF16)
    terms = lax.dot_general(
        data, images, (((0,), (0,)), ((), ())), preferred_element_type=F32
    )
    row_total = (jnp.sum(block_counts) * BLOCK).astype(F32)
    updated = basis.astype(F32) + total(terms, "dp") / row_total
    first_basis, upper_one = orthonormal(updated)
    second_basis, upper_two = orthonormal(first_basis)
    upper = jnp.dot(upper_two, upper_one, precision=lax.Precision.HIGHEST)
    return (second_basis * math.sqrt(D), upper)


def on_device(data, block_counts, basis):
    rows, columns = data.shape
    rank = basis.shape[1]
    dp = lax.axis_index("dp")
    feat = lax.axis_index("feat")
    dp_size = lax.axis_size("dp")
    active = lax.dynamic_index_in_dim(block_counts, dp, 0, False)
    terms = column_terms(data, basis, active, feat % CORES)
    pieces = lax.all_to_all(terms.reshape(dp_size, columns // dp_size, rank), "dp", 0, 0)
    piece = (jnp.sum(pieces.astype(F32), axis=0) * (LIFT_STEP / LIFT)).astype(F16)
    step = spread(piece, "dp", None, dp_size).reshape(columns, rank).astype(F32)
    updated, mine, theirs = gram_share(block_counts, step, basis)
    gram, data, block_counts, basis = lax.optimization_barrier(
        (sum_gram(mine, theirs), data, block_counts, basis)
    )
    basis_scaled, upper, done = factor(gram, updated)
    return lax.cond(
        done[0] == 1,
        lambda: (basis_scaled, upper),
        lambda: general(data, block_counts, basis),
    )


def solution(mesh):
    in_specs = (P("dp", "feat"), P(), P("feat", None))
    out_specs = (P("feat", None), P())
    return jax.shard_map(
        on_device, mesh=mesh, in_specs=in_specs, out_specs=out_specs, check_vma=False
    )
```
